32 devices in a mesh: col: 8 (over z, y), row: 4 (over x, core).
Axes of the slice: x: 2, y: 2, z: 4, core: 2. Of those that a mesh axis runs over, the one named last changes fastest.
Arguments:
- panel: int32 [8], replicated, may hold values from 0 to 7, each once
- centres_cols: bfloat16 [4096, 1024], P('col'), may hold values from -1 to 1
- centres_rows: bfloat16 [128, 1024], P(('row', 'col')), may hold values from -1 to 1
- diag_inverse: float32 [4096, 512], P('col'), as said below
- trailing: float32 [128, 4096], P('row', 'col'), may hold values from -6 to 6
Outputs:
- updated: float32 [128, 4096], P('row', 'col')
The draws below stay inside these ranges and needn't reach their ends.
Inputs may be any that keep to these rules, and one draw needn't show every extreme that they name: panel holds each of 0 to 7 once. Each 512 x 512 block of diag_inverse is lower triangular with a positive diagonal.
All inputs are finite; a program needn't handle non-finite values.
Results may differ from the reference program's by a relative error of at most 0.0003.
Values may be sent and summed in bfloat16 or wider, within the bound.
A program may use at most 64 MiB of HBM per device.

```python
import math
import jax
import jax.numpy as jnp
from jax import lax

D = 1024
BLK = 512
LAYERS = 3
ROWS = 128
BLOCKS = 8
COLS = 4096
RANK = 2


def centre_law(key, total, salt):
    shared = jax.random.fold_in(key, 7)
    key_mean, key_cent, key_weight = jax.random.split(shared, 3)
    clusters = max(BLK // 4, 4)
    mean_dir = jax.random.normal(key_mean, (D,), jnp.float32)
    centroids = jax.random.normal(key_cent, (clusters, D), jnp.float32)
    weights = jax.random.uniform(key_weight, (clusters,), jnp.float32, 0.5, 1.5)
    own_key = jax.random.fold_in(key, salt)
    key_assign, key_jitter, key_scale = jax.random.split(own_key, 3)
    member = jax.random.randint(key_assign, (total,), 0, clusters)
    jitter = jax.random.normal(key_jitter, (total, D), jnp.float32)
    row_scale = jnp.exp(jax.random.uniform(key_scale, (total,), jnp.float32, -0.6931472, 0.6931472))
    values = weights[member][:, None] * mean_dir[None, :] + 0.7 * centroids[member] + 0.45 * jitter
    values = values * (row_scale / jnp.sqrt(jnp.float32(D)))[:, None]
    return jnp.clip(values, -1.0, 1.0).astype(jnp.bfloat16)


def draw_centres_cols(key, part):
    return centre_law(key, COLS, 1)


def draw_centres_rows(key, part):
    return centre_law(key, ROWS, 2)


def draw_diag_inverse(key, part):
    key_off, key_diag = jax.random.split(key)
    blocks_all = COLS // BLK
    off_diag = jax.random.normal(key_off, (blocks_all, BLK, BLK), jnp.float32) * 0.05
    diag_vals = jax.random.uniform(key_diag, (blocks_all, BLK), jnp.float32, 1.0, 2.0)
    identity = jnp.eye(BLK, dtype=jnp.float32)
    lower = jnp.tril(off_diag, -1) + diag_vals[:, :, None] * identity[None, :, :]
    return (lower / jnp.sqrt(jnp.float32(BLK))).reshape(COLS, BLK)


def levels(stream_key, dims, shards, smallest, top_value):
    def one(position, parts):
        heights = jax.random.uniform(jax.random.fold_in(jax.random.fold_in(stream_key, 6), position), (parts,), jnp.float32, smallest / len(shards), top_value / len(shards))
        return jnp.repeat(jnp.exp(heights), dims[position] // parts).reshape((-1,) + (1,) * (len(dims) - position - 1))

    gain = one(*shards[0])
    for cut in shards[1:]:
        gain = gain * one(*cut)
    return gain


def scatter_about(rng, shape, scale, most, pieces=(), kind=jnp.bfloat16):
    loudness = levels(rng, shape, pieces, -0.22, 0.18) if pieces else 1.0
    drawn = jax.random.normal(rng, shape, jnp.float32) * scale * loudness
    return jnp.minimum(jnp.maximum(drawn, -most), most).astype(kind)


def setup_inputs(seed: int = 0) -> dict:
    keys = jax.random.split(jax.random.key(seed), 6)
    return {
        "panel": jax.random.permutation(keys[0], BLOCKS).astype(jnp.int32),
        "centres_cols": draw_centres_cols(jax.random.fold_in(keys[5], 71), 0),
        "centres_rows": draw_centres_rows(jax.random.fold_in(keys[5], 71), 0),
        "diag_inverse": draw_diag_inverse(jax.random.fold_in(keys[5], 71), 0),
        "trailing": scatter_about(keys[4], (ROWS, COLS), 1.0, 6.0, ((0, 4), (1, 8)), jnp.float32),
    }


def kernel(left, right):
    gram = lax.dot_general(left, right, (((1,), (1,)), ((), ())), preferred_element_type=jnp.float32)
    left_f = left.astype(jnp.float32)
    right_f = right.astype(jnp.float32)
    inv_left = 1.0 / jnp.sqrt(lax.optimization_barrier(jnp.sum(left_f * left_f, axis=1)) + 1e-06)
    inv_right = 1.0 / jnp.sqrt(lax.optimization_barrier(jnp.sum(right_f * right_f, axis=1)) + 1e-06)
    cosine = gram * inv_left[:, None] * inv_right[None, :]
    theta = cosine
    rho_now = cosine
    for layer in range(LAYERS):
        angle_now = jnp.arccos(rho_now)
        zero_order = (math.pi - angle_now) / math.pi
        rho_next = (jnp.sqrt(1.0 - rho_now * rho_now) + (math.pi - angle_now) * rho_now) / math.pi
        theta = theta * zero_order + rho_next
        rho_now = rho_next
    return theta / (inv_left[:, None] * inv_right[None, :])

def apply_inverse(values, inverse):
    return lax.dot_general(values, inverse, (((1,), (1,)), ((), ())), precision=lax.Precision.HIGHEST, preferred_element_type=jnp.float32)

def reference(panel, centres_cols, centres_rows, diag_inverse, trailing):
    block_ids = jnp.arange(BLOCKS, dtype=jnp.int32)
    panel_at = jnp.sum(jnp.where(panel == RANK, block_ids, 0)).astype(jnp.int32)
    start = (panel_at * BLK).astype(jnp.int32)
    panel_x = lax.dynamic_slice_in_dim(centres_cols, start, BLK, 0)
    panel_inv = lax.dynamic_slice_in_dim(diag_inverse, start, BLK, 0)
    rows_l = apply_inverse(kernel(centres_rows, panel_x), panel_inv)
    cols_l = apply_inverse(kernel(centres_cols, panel_x), panel_inv)
    update = lax.dot_general(rows_l, cols_l, (((1,), (1,)), ((), ())), precision=lax.Precision.HIGHEST, preferred_element_type=jnp.float32)
    later = jnp.repeat(panel > RANK, BLK)
    return jnp.where(later[None, :], trailing - update, trailing)
```

```python
import functools
import math

import jax
import jax.numpy as jnp
from jax import lax
from jax.experimental import pallas as pl
from jax.experimental.pallas import tpu as pltpu
from jax.sharding import PartitionSpec as P

LAYERS = 3
EPS = 1e-06
CHUNKS = 4
MESH = pl.DeviceIdType.MESH
F32 = jnp.float32
BF16 = jnp.bfloat16
ACOS = tuple(
    v / math.pi
    for v in (
        1.5707963050, -0.2145988016, 0.0889789874, -0.0501743046,
        0.0308918810, -0.0170881256, 0.0066700901, -0.0012624911,
    )
)


def root(y):
    y = jnp.maximum(y, 1e-30)
    return y * lax.rsqrt(y)


def theta_of(u):
    rho = jnp.clip(u, -1.0, 1.0)
    theta = rho
    for layer in range(LAYERS):
        size = jnp.abs(rho) if layer == 0 else rho
        poly = jnp.full_like(size, ACOS[-1])
        for coef in ACOS[-2::-1]:
            poly = poly * size + coef
        low = root(1.0 - size)
        angle = low * poly
        sine = low * root(1.0 + size)
        if layer == 0:
            zero_order = jnp.where(rho < 0.0, angle, 1.0 - angle)
        else:
            zero_order = 1.0 - angle
        rho_next = sine * (1.0 / math.pi) + zero_order * rho
        theta = theta * zero_order + rho_next
        rho = rho_next
    return theta


def dot_t(a, b, precision=None):
    return lax.dot_general(
        a, b, (((1,), (1,)), ((), ())), precision=precision, preferred_element_type=F32
    )


def kernel(
    n, nr, panel, x_ref, rows_ref, inv_ref, trail_ref, out_ref,
    rows_buf, rows_all, py, pr, plft, w_out, wy, wr, wl, kt, part, part_in,
    rows_send, rows_recv, py_send, py_recv, pz_send, pz_recv,
    wx_send, wx_recv, wy_send, wy_recv, wz_send, wz_recv, pt_send, pt_recv,
):
    col = lax.axis_index("col")
    row = lax.axis_index("row")
    nz = n // 2
    z, y = col // 2, col % 2
    y_mate = z * 2 + 1 - y
    right, left = lax.rem(col + 2, n), lax.rem(col + n - 2, n)
    blk = x_ref.shape[0]
    quarter = blk // nr
    size = quarter // CHUNKS
    per = rows_ref.shape[0]
    group = per * n

    target = n // 4
    at = jnp.int32(0)
    for i in range(n):
        at = at + jnp.where(panel[i] == target, i, 0)
    root_here = at == col
    root_layer = at // 2 == z
    from_left = at // 2 <= z

    barrier = pltpu.get_barrier_semaphore()
    for d in range(1, n):
        pl.semaphore_signal(
            barrier, inc=1, device_id={"col": lax.rem(col + d, n)}, device_id_type=MESH
        )
    for d in range(1, nr):
        pl.semaphore_signal(
            barrier, inc=1, device_id={"row": lax.rem(row + d, nr)}, device_id_type=MESH
        )
    rows_buf[col] = rows_ref[...].astype(F32)
    pl.semaphore_wait(barrier, n - 1 + nr - 1)

    def remote(src, dst, send, recv, **where):
        return pltpu.make_async_remote_copy(
            src_ref=src, dst_ref=dst, send_sem=send, recv_sem=recv,
            device_id=where, device_id_type=MESH,
        )

    def rows_copy(d, slot):
        return remote(
            rows_buf.at[slot], rows_buf.at[slot], rows_send.at[d], rows_recv.at[slot],
            col=lax.rem(col + d, n),
        )

    for d in range(1, n):
        rows_copy(d, col).start()

    def own_chunk(k):
        return pl.ds(pl.multiple_of(row * quarter + k * size, size), size)

    def py_copy(k):
        return remote(x_ref.at[own_chunk(k)], py.at[k], py_send.at[k], py_recv.at[k], col=y_mate)

    for k in range(CHUNKS):
        py_copy(k).start()

    xf = x_ref[...].astype(F32)
    sq = xf * xf
    sq_hi = sq.astype(BF16)
    sq_lo = (sq - sq_hi.astype(F32)).astype(BF16)
    ones = jnp.ones((16, x_ref.shape[1]), BF16)
    x_sum = (dot_t(ones, sq_hi) + dot_t(ones, sq_lo))[0:1, :] + EPS
    x_norm = jnp.sqrt(x_sum)
    x_inv = 1.0 / x_norm

    def block_kernel(a, a_f):
        a_norm = jnp.sqrt(jnp.sum(a_f * a_f, axis=1, keepdims=True) + EPS)
        u = dot_t(a, x_ref[...]) * (1.0 / a_norm) * x_inv
        return theta_of(u) * (a_norm * x_norm)

    def z_copy(buf, k, way, send, recv):
        return remote(
            buf.at[k], buf.at[k], send.at[way, k], recv.at[way, k],
            col=right if way == 0 else left,
        )

    def flood(step, units, cand, bufs, send, recv):
        for way in (0, 1):
            pos = z if way == 0 else nz - 1 - z
            k = step - pos
            buf = bufs[way]

            @pl.when(jnp.logical_and(k >= 0, k < units))
            def _():
                @pl.when(pos == 0)
                def _():
                    buf[k] = cand(k)

                @pl.when(pos > 0)
                def _():
                    z_copy(buf, k, way, send, recv).wait_recv()
                    buf[k] = lax.select(root_layer, cand(k), buf[k])

                @pl.when(pos < nz - 1)
                def _():
                    z_copy(buf, k, way, send, recv).start()

    def flood_end(units, bufs, send, recv):
        for way in (0, 1):
            pos = z if way == 0 else nz - 1 - z

            @pl.when(pos < nz - 1)
            def _():
                for k in range(units):
                    z_copy(bufs[way], k, way, send, recv).wait_send()

    def panel_cand(k):
        return py[k]

    def panel_step(step):
        if step < CHUNKS:
            py_copy(step).wait_recv()
            own = x_ref[own_chunk(step), :]
            py[step] = lax.select(root_here, own, py[step])
        flood(step, CHUNKS, panel_cand, (pr, plft), pz_send, pz_recv)
        k = step - (nz - 1)
        if k >= 0:
            chunk = lax.select(from_left, pr[k], plft[k])
            kt[k * size:(k + 1) * size, :] = block_kernel(chunk, chunk.astype(F32))

    def work_rows():
        for d in range(1, n):
            slot = lax.rem(col + n - d, n)
            rows_copy(d, slot).wait_recv()
        for c in range(n):
            rows_all[c * per:(c + 1) * per, :] = rows_buf[c]
        a_f = rows_all[...]
        return block_kernel(a_f.astype(BF16), a_f)

    def wx_copy(d, slot):
        return remote(
            w_out.at[lax.rem(row + d, nr)], wy.at[nr + slot], wx_send.at[d], wx_recv.at[slot],
            row=lax.rem(row + d, nr),
        )

    def wy_copy(k):
        return remote(wy.at[nr + k], wy.at[k], wy_send.at[k], wy_recv.at[k], col=y_mate)

    def work_w(mid):
        w = jnp.dot(mid, inv_ref[...], precision=lax.Precision.HIGHEST, preferred_element_type=F32)
        for j in range(nr):
            w_out[j] = w[:, j * quarter:(j + 1) * quarter]
        for d in range(1, nr):
            wx_copy(d, row).start()
        wy[nr + row] = w_out[row]

    def work_exchange():
        for d in range(1, nr):
            wx_copy(d, lax.rem(row + nr - d, nr)).wait_recv()
        for k in range(nr):
            wy_copy(k).start()

    def w_step(step):
        if step < nr:
            wy_copy(step).wait_recv()
            wy[step] = lax.select(root_here, wy[nr + step], wy[step])
        flood(step, nr, lambda k: wy[k], (wr, wl), wz_send, wz_recv)

    panel_steps = CHUNKS + nz - 1
    w_steps = nr + nz - 1
    todo = list(range(panel_steps))
    k_rows = work_rows()
    panel_step(todo.pop(0))
    mid = dot_t(k_rows, inv_ref[...], lax.Precision.HIGHEST)
    panel_step(todo.pop(0))
    work_w(mid)
    panel_step(todo.pop(0))
    panel_step(todo.pop(0))
    work_exchange()
    for step in range(w_steps):
        if todo:
            panel_step(todo.pop(0))
        w_step(step)
    while todo:
        panel_step(todo.pop(0))

    def part_copy(d, slot):
        return remote(
            part.at[lax.rem(row + d, nr)], part_in.at[slot], pt_send.at[d], pt_recv.at[slot],
            row=lax.rem(row + d, nr),
        )

    for j in range(nr):
        w = lax.select(from_left, wr[j], wl[j])
        part[j] = jnp.dot(w, kt[...], precision=lax.Precision.HIGHEST, preferred_element_type=F32)
    for d in range(1, nr):
        part_copy(d, row).start()
    total = part[row]
    for d in range(1, nr):
        slot = lax.rem(row + nr - d, nr)
        part_copy(d, slot).wait_recv()
        total = total + part_in[slot]
    trail = trail_ref[...]
    out_ref[...] = lax.select(panel[col] > target, trail - total, trail)

    for d in range(1, n):
        rows_copy(d, col).wait_send()
    for k in range(CHUNKS):
        py_copy(k).wait_send()
    for d in range(1, nr):
        wx_copy(d, row).wait_send()
        part_copy(d, row).wait_send()
    for k in range(nr):
        wy_copy(k).wait_send()
    flood_end(CHUNKS, (pr, plft), pz_send, pz_recv)
    flood_end(nr, (wr, wl), wz_send, wz_recv)


def on_device(n, nr, panel, centres_cols, centres_rows, diag_inverse, trailing):
    blk, width = centres_cols.shape
    quarter = blk // nr
    size = quarter // CHUNKS
    per = centres_rows.shape[0]
    group = per * n
    dma = pltpu.SemaphoreType.DMA
    vmem = pl.BlockSpec(memory_space=pltpu.VMEM)
    return pl.pallas_call(
        functools.partial(kernel, n, nr),
        out_shape=jax.ShapeDtypeStruct(trailing.shape, F32),
        in_specs=[pl.BlockSpec(memory_space=pltpu.SMEM)] + [vmem] * 4,
        out_specs=vmem,
        scratch_shapes=[
            pltpu.VMEM((n, per, width), F32),
            pltpu.VMEM((group, width), F32),
            pltpu.VMEM((CHUNKS, size, width), BF16),
            pltpu.VMEM((CHUNKS, size, width), BF16),
            pltpu.VMEM((CHUNKS, size, width), BF16),
            pltpu.VMEM((nr, group, quarter), F32),
            pltpu.VMEM((2 * nr, group, quarter), F32),
            pltpu.VMEM((nr, group, quarter), F32),
            pltpu.VMEM((nr, group, quarter), F32),
            pltpu.VMEM((quarter, blk), F32),
            pltpu.VMEM((nr, group, blk), F32),
            pltpu.VMEM((nr, group, blk), F32),
            dma((n,)), dma((n,)),
            dma((CHUNKS,)), dma((CHUNKS,)),
            dma((2, CHUNKS)), dma((2, CHUNKS)),
            dma((nr,)), dma((nr,)),
            dma((nr,)), dma((nr,)),
            dma((2, nr)), dma((2, nr)),
            dma((nr,)), dma((nr,)),
        ],
        compiler_params=pltpu.CompilerParams(
            collective_id=0, has_side_effects=True, vmem_limit_bytes=48 * 2**20
        ),
    )(panel, centres_cols, centres_rows, diag_inverse, trailing)


def solution(mesh):
    return jax.shard_map(
        functools.partial(on_device, mesh.shape["col"], mesh.shape["row"]),
        mesh=mesh,
        in_specs=(P(), P("col", None), P(("row", "col"), None), P("col", None), P("row", "col")),
        out_specs=P("row", "col"),
        check_vma=False,
    )
```

```python
import functools
import math

import jax
import jax.numpy as jnp
from jax import lax
from jax.experimental import pallas as pl
from jax.experimental.pallas import tpu as pltpu
from jax.sharding import PartitionSpec as P

LAYERS = 3
EPS = 1e-06
UNITS = 8
GROUPS = 2
HOP = 2
MESH = pl.DeviceIdType.MESH
F32 = jnp.float32
BF16 = jnp.bfloat16
ACOS = tuple(
    v / math.pi
    for v in (
        1.5707963050, -0.2145988016, 0.0889789874, -0.0501743046,
        0.0308918810, -0.0170881256, 0.0066700901, -0.0012624911,
    )
)


def root(y):
    y = jnp.maximum(y, 1e-30)
    return y * lax.rsqrt(y)


def theta_of(u):
    rho = jnp.clip(u, -1.0, 1.0)
    theta = rho
    for layer in range(LAYERS):
        size = jnp.abs(rho) if layer == 0 else rho
        poly = jnp.full_like(size, ACOS[-1])
        for coef in ACOS[-2::-1]:
            poly = poly * size + coef
        low = root(1.0 - size)
        angle = low * poly
        sine = low * root(1.0 + size)
        if layer == 0:
            zero_order = jnp.where(rho < 0.0, angle, 1.0 - angle)
        else:
            zero_order = 1.0 - angle
        rho_next = sine * (1.0 / math.pi) + zero_order * rho
        theta = theta * zero_order + rho_next
        rho = rho_next
    return theta


def dot_t(a, b, precision=None):
    return lax.dot_general(
        a, b, (((1,), (1,)), ((), ())), precision=precision, preferred_element_type=F32
    )


def split3(a):
    hi = a.astype(BF16)
    rest = a - hi.astype(F32)
    mid = rest.astype(BF16)
    return hi, mid, (rest - mid.astype(F32)).astype(BF16)


def product3(a, weights, transposed):
    m = a.shape[0]
    terms = jnp.concatenate(split3(a), axis=0)
    dims = (((1,), (1 if transposed else 0,)), ((), ()))

    def mul(count, w):
        return lax.dot_general(terms[:count * m], w, dims, preferred_element_type=F32)

    p, q, t = mul(3, weights[0]), mul(2, weights[1]), mul(1, weights[2])
    small = t + q[m:] + p[2 * m:]
    return (small + (q[:m] + p[m:2 * m])) + p[:m]


def kernel(
    n, nr, panel_hbm, x_hbm, rows_ref, inv_hbm, trail_hbm, out_ref,
    panel, x_ref, inv_ref, trail_ref,
    rows_buf, rows_all, inv3, py, pr, plft, w_out, wo, wm, wr, wl, kt, part, part_in,
    in_sem, rows_send, rows_recv, py_send, py_recv, pz_send, pz_recv,
    wo_send, wo_recv, wm_send, wm_recv, wz_send, wz_recv, pt_send, pt_recv,
):
    col = lax.axis_index("col")
    row = lax.axis_index("row")
    nz = n // 2
    z, y = col // 2, col % 2
    y_mate = z * 2 + 1 - y
    right, left = lax.rem(col + 2, n), lax.rem(col + n - 2, n)
    blk, width = x_ref.shape
    half = blk // 2
    quarter = blk // nr
    size = quarter // UNITS
    per = rows_ref.shape[0]

    barrier = pltpu.get_barrier_semaphore()

    def greet(**where):
        pl.semaphore_signal(barrier, inc=1, device_id=where, device_id_type=MESH)

    for d in range(1, n):
        greet(col=lax.rem(col + d, n))
    for d in range(1, nr):
        greet(row=lax.rem(row + d, nr))
        greet(row=lax.rem(row + d, nr), col=y_mate)
    loads = [
        pltpu.make_async_copy(src, dst, in_sem.at[i])
        for i, (src, dst) in enumerate(
            ((panel_hbm, panel), (x_hbm, x_ref), (inv_hbm, inv_ref), (trail_hbm, trail_ref))
        )
    ]
    for load in loads:
        load.start()
    rows_buf[col] = rows_ref[...].astype(F32)
    pl.semaphore_wait(barrier, n - 1 + 2 * (nr - 1))

    def remote(src, dst, send, recv, **where):
        return pltpu.make_async_remote_copy(
            src_ref=src, dst_ref=dst, send_sem=send, recv_sem=recv,
            device_id=where, device_id_type=MESH,
        )

    def rows_copy(d, slot):
        return remote(
            rows_buf.at[slot], rows_buf.at[slot], rows_send.at[d], rows_recv.at[slot],
            col=lax.rem(col + d, n),
        )

    for d in range(1, n):
        rows_copy(d, col).start()

    def unit(k):
        return pl.ds(pl.multiple_of(k * size, size), size)

    def own_unit(k):
        return pl.ds(pl.multiple_of(row * quarter + k * size, size), size)

    def py_copy(k):
        return remote(
            x_hbm.at[own_unit(k)], py.at[unit(k)], py_send.at[k], py_recv.at[k], col=y_mate
        )

    for k in range(UNITS):
        py_copy(k).start()
    for load in loads:
        load.wait()

    target = n // 4
    at = jnp.int32(0)
    for i in range(n):
        at = at + jnp.where(panel[i] == target, i, 0)
    root_here = at == col
    root_layer = at // 2 == z
    from_left = at // 2 <= z

    sums = jnp.zeros((blk, 128), F32)
    for j in range(0, width, 128):
        piece = x_ref[:, j:j + 128].astype(F32)
        sums = sums + piece * piece
    x_norm = jnp.sqrt(jnp.sum(sums.T, axis=0, keepdims=True) + EPS)
    x_inv = 1.0 / x_norm
    for i, term in enumerate(split3(inv_ref[...])):
        inv3[i] = term

    def block_kernel(a, a_f):
        a_norm = jnp.sqrt(jnp.sum(a_f * a_f, axis=1, keepdims=True) + EPS)
        u = dot_t(a, x_ref[...]) * (1.0 / a_norm) * x_inv
        return theta_of(u) * (a_norm * x_norm)

    def z_copy(buf, index, k, way, send, recv):
        return remote(
            buf.at[index], buf.at[index], send.at[way, k], recv.at[way, k],
            col=right if way == 0 else left,
        )

    def position(way):
        return z if way == 0 else nz - 1 - z

    def pass_on(buf, index, k, way, cand, send, recv):
        pos = position(way)

        @pl.when(pos == 0)
        def _():
            buf[index] = cand()

        @pl.when(pos > 0)
        def _():
            z_copy(buf, index, k, way, send, recv).wait_recv()
            buf[index] = lax.select(root_layer, cand(), buf[index])

        @pl.when(pos < nz - 1)
        def _():
            z_copy(buf, index, k, way, send, recv).start()

    def panel_slot(step):
        @pl.when(step < UNITS)
        def _():
            py_copy(step).wait_recv()
            own = x_ref[own_unit(step), :]
            py[unit(step), :] = lax.select(root_here, own, py[unit(step), :])

        for way, buf in enumerate((pr, plft)):
            k = step - HOP * position(way)

            @pl.when(jnp.logical_and(k >= 0, k < UNITS))
            def _():
                pass_on(buf, unit(k), k, way, lambda: py[unit(k), :], pz_send, pz_recv)

    def slots(first, last):
        @pl.loop(first, last)
        def _(step):
            panel_slot(step)

    def panel_group(g):
        sel = slice(g * quarter // GROUPS, (g + 1) * quarter // GROUPS)
        a = lax.select(from_left, pr[sel, :], plft[sel, :])
        kt[sel, :] = block_kernel(a, a.astype(F32))

    def work_rows():
        for d in range(1, n):
            slot = lax.rem(col + n - d, n)
            rows_copy(d, slot).wait_recv()
        for c in range(n):
            rows_all[c * per:(c + 1) * per, :] = rows_buf[c]
        a_f = rows_all[...]
        return block_kernel(a_f.astype(BF16), a_f)

    def wo_copy(d, slot):
        peer = lax.rem(row + d, nr)
        return remote(w_out.at[peer], wo.at[slot], wo_send.at[d], wo_recv.at[slot], row=peer)

    def wm_copy(d, slot):
        peer = lax.rem(row + d, nr)
        return remote(
            w_out.at[peer], wm.at[slot], wm_send.at[d], wm_recv.at[slot], row=peer, col=y_mate
        )

    def work_mid(a):
        low = product3(a[:, :half], [inv3[i, :half, :half] for i in range(3)], True)
        high = product3(a, [inv3[i, half:, :] for i in range(3)], True)
        return jnp.concatenate([low, high], axis=1)

    def work_w(mid):
        low = product3(mid, [inv3[i, :, :half] for i in range(3)], False)
        high = product3(mid[:, half:], [inv3[i, half:, half:] for i in range(3)], False)
        w = jnp.concatenate([low, high], axis=1)
        for j in range(nr):
            w_out[j] = w[:, j * quarter:(j + 1) * quarter]
        for d in range(nr):
            wm_copy(d, row).start()
        for d in range(1, nr):
            wo_copy(d, row).start()
        wo[row] = w_out[row]

    def work_exchange():
        for d in range(nr):
            slot = lax.rem(row + nr - d, nr)
            wm_copy(d, slot).wait_recv()
        for d in range(1, nr):
            slot = lax.rem(row + nr - d, nr)
            wo_copy(d, slot).wait_recv()
        for k in range(nr):
            wm[k] = lax.select(root_here, wo[k], wm[k])

    def w_hop(step):
        for way, buf in enumerate((wr, wl)):
            @pl.when(position(way) == step)
            def _():
                for k in range(nr):
                    pass_on(buf, k, k, way, lambda: wm[k], wz_send, wz_recv)

    last = UNITS + HOP * (nz - 1)
    first_group = last - UNITS + UNITS // GROUPS
    slots(0, 2)
    k_rows = work_rows()
    slots(2, 4)
    mid = work_mid(k_rows)
    slots(4, 6)
    work_w(mid)
    slots(6, first_group)
    work_exchange()
    w_hop(0)
    panel_group(0)
    for g in range(1, GROUPS):
        slots(first_group + (g - 1) * UNITS // GROUPS, first_group + g * UNITS // GROUPS)
        w_hop(g)
        panel_group(g)

    @pl.loop(GROUPS, nz)
    def _(step):
        w_hop(step)

    def part_copy(d, slot):
        peer = lax.rem(row + d, nr)
        return remote(part.at[peer], part_in.at[slot], pt_send.at[d], pt_recv.at[slot], row=peer)

    w = jnp.concatenate([lax.select(from_left, wr[j], wl[j]) for j in range(nr)], axis=0)
    update = jnp.dot(w, kt[...], precision=lax.Precision.HIGHEST, preferred_element_type=F32)
    group = update.shape[0] // nr
    for j in range(nr):
        part[j] = update[j * group:(j + 1) * group]
    for d in range(1, nr):
        part_copy(d, row).start()
    total = part[row]
    for d in range(1, nr):
        slot = lax.rem(row + nr - d, nr)
        part_copy(d, slot).wait_recv()
        total = total + part_in[slot]
    trail = trail_ref[...]
    out_ref[...] = lax.select(panel[col] > target, trail - total, trail)

    for d in range(1, n):
        rows_copy(d, col).wait_send()
    for k in range(UNITS):
        py_copy(k).wait_send()
    for d in range(nr):
        wm_copy(d, row).wait_send()
    for d in range(1, nr):
        wo_copy(d, row).wait_send()
        part_copy(d, row).wait_send()
    for way in (0, 1):
        @pl.when(position(way) < nz - 1)
        def _():
            for k in range(UNITS):
                z_copy((pr, plft)[way], unit(k), k, way, pz_send, pz_recv).wait_send()
            for k in range(nr):
                z_copy((wr, wl)[way], k, k, way, wz_send, wz_recv).wait_send()


def on_device(n, nr, panel, centres_cols, centres_rows, diag_inverse, trailing):
    blk, width = centres_cols.shape
    quarter = blk // nr
    per = centres_rows.shape[0]
    group = per * n
    dma = pltpu.SemaphoreType.DMA
    vmem = pl.BlockSpec(memory_space=pltpu.VMEM)
    hbm = pl.BlockSpec(memory_space=pltpu.HBM)
    return pl.pallas_call(
        functools.partial(kernel, n, nr),
        out_shape=jax.ShapeDtypeStruct(trailing.shape, F32),
        in_specs=[hbm, hbm, vmem, hbm, hbm],
        out_specs=vmem,
        scratch_shapes=[
            pltpu.SMEM(panel.shape, jnp.int32),
            pltpu.VMEM(centres_cols.shape, BF16),
            pltpu.VMEM(diag_inverse.shape, F32),
            pltpu.VMEM(trailing.shape, F32),
            pltpu.VMEM((n, per, width), F32),
            pltpu.VMEM((group, width), F32),
            pltpu.VMEM((3, blk, blk), BF16),
            pltpu.VMEM((quarter, width), BF16),
            pltpu.VMEM((quarter, width), BF16),
            pltpu.VMEM((quarter, width), BF16),
            pltpu.VMEM((nr, group, quarter), F32),
            pltpu.VMEM((nr, group, quarter), F32),
            pltpu.VMEM((nr, group, quarter), F32),
            pltpu.VMEM((nr, group, quarter), F32),
            pltpu.VMEM((nr, group, quarter), F32),
            pltpu.VMEM((quarter, blk), F32),
            pltpu.VMEM((nr, group, blk), F32),
            pltpu.VMEM((nr, group, blk), F32),
            dma((4,)),
            dma((n,)), dma((n,)),
            dma((UNITS,)), dma((UNITS,)),
            dma((2, UNITS)), dma((2, UNITS)),
            dma((nr,)), dma((nr,)),
            dma((nr,)), dma((nr,)),
            dma((2, nr)), dma((2, nr)),
            dma((nr,)), dma((nr,)),
        ],
        compiler_params=pltpu.CompilerParams(
            collective_id=0, has_side_effects=True, vmem_limit_bytes=48 * 2**20
        ),
    )(panel, centres_cols, centres_rows, diag_inverse, trailing)


def solution(mesh):
    return jax.shard_map(
        functools.partial(on_device, mesh.shape["col"], mesh.shape["row"]),
        mesh=mesh,
        in_specs=(P(), P("col", None), P(("row", "col"), None), P("col", None), P("row", "col")),
        out_specs=P("row", "col"),
        check_vma=False,
    )
```

```python
import functools
import math

import jax
import jax.numpy as jnp
from jax import lax
from jax.experimental import pallas as pl
from jax.experimental.pallas import tpu as pltpu
from jax.sharding import PartitionSpec as P

LAYERS = 3
EPS = 1e-06
UNITS = 8
GROUPS = 2
HOP = 3
VMEM_BYTES = 63 * 2**20
MESH = pl.DeviceIdType.MESH
F32 = jnp.float32
BF16 = jnp.bfloat16
ACOS = tuple(
    v / math.pi
    for v in (
        1.5707963050, -0.2145988016, 0.0889789874, -0.0501743046,
        0.0308918810, -0.0170881256, 0.0066700901, -0.0012624911,
    )
)


def root(y):
    y = jnp.maximum(y, 1e-30)
    return y * lax.rsqrt(y)


def theta_of(u):
    rho = jnp.clip(u, -1.0, 1.0)
    theta = rho
    for layer in range(LAYERS):
        size = jnp.abs(rho) if layer == 0 else rho
        poly = jnp.full_like(size, ACOS[-1])
        for coef in ACOS[-2::-1]:
            poly = poly * size + coef
        low = root(1.0 - size)
        angle = low * poly
        sine = low * root(1.0 + size)
        if layer == 0:
            zero_order = jnp.where(rho < 0.0, angle, 1.0 - angle)
        else:
            zero_order = 1.0 - angle
        rho_next = sine * (1.0 / math.pi) + zero_order * rho
        theta = theta * zero_order + rho_next
        rho = rho_next
    return theta


def dot_t(a, b, precision=None):
    return lax.dot_general(
        a, b, (((1,), (1,)), ((), ())), precision=precision, preferred_element_type=F32
    )


def split3(a):
    hi = a.astype(BF16)
    rest = a - hi.astype(F32)
    mid = rest.astype(BF16)
    return hi, mid, (rest - mid.astype(F32)).astype(BF16)


def product3(a, weights, transposed):
    m = a.shape[0]
    terms = jnp.concatenate(split3(a), axis=0)
    dims = (((1,), (1 if transposed else 0,)), ((), ()))

    def mul(count, w):
        return lax.dot_general(terms[:count * m], w, dims, preferred_element_type=F32)

    p, q, t = mul(3, weights[0]), mul(2, weights[1]), mul(1, weights[2])
    small = t + q[m:] + p[2 * m:]
    return (small + (q[:m] + p[m:2 * m])) + p[:m]


def kernel(
    n, nr, panel_hbm, x_hbm, rows_ref, inv_hbm, trail_hbm, out_ref,
    panel, x_ref, inv_ref, trail_ref,
    rows_buf, rows_all, inv3, py, pr, plft, w_out, wo, wm, wr, wl, kt, part, part_in,
    in_sem, rows_send, rows_recv, py_send, py_recv, pz_send, pz_recv,
    wo_send, wo_recv, wm_send, wm_recv, wz_send, wz_recv, pt_send, pt_recv,
):
    col = lax.axis_index("col")
    row = lax.axis_index("row")
    nz = n // 2
    z, y = col // 2, col % 2
    y_mate = z * 2 + 1 - y
    right, left = lax.rem(col + 2, n), lax.rem(col + n - 2, n)
    blk, width = x_ref.shape
    half = blk // 2
    quarter = blk // nr
    size = quarter // UNITS
    per = rows_ref.shape[0]

    barrier = pltpu.get_barrier_semaphore()

    def greet(**where):
        pl.semaphore_signal(barrier, inc=1, device_id=where, device_id_type=MESH)

    for d in range(1, n):
        greet(col=lax.rem(col + d, n))
    for d in range(1, nr):
        greet(row=lax.rem(row + d, nr))
        greet(row=lax.rem(row + d, nr), col=y_mate)
    loads = [
        pltpu.make_async_copy(src, dst, in_sem.at[i])
        for i, (src, dst) in enumerate(
            ((panel_hbm, panel), (x_hbm, x_ref), (inv_hbm, inv_ref), (trail_hbm, trail_ref))
        )
    ]
    for load in loads:
        load.start()
    rows_buf[col] = rows_ref[...].astype(F32)
    pl.semaphore_wait(barrier, n - 1 + 2 * (nr - 1))

    def remote(src, dst, send, recv, **where):
        return pltpu.make_async_remote_copy(
            src_ref=src, dst_ref=dst, send_sem=send, recv_sem=recv,
            device_id=where, device_id_type=MESH,
        )

    def rows_copy(d, slot):
        return remote(
            rows_buf.at[slot], rows_buf.at[slot], rows_send.at[d], rows_recv.at[slot],
            col=lax.rem(col + d, n),
        )

    for d in range(1, n):
        rows_copy(d, col).start()

    def unit(k):
        return pl.ds(pl.multiple_of(k * size, size), size)

    def own_unit(k):
        return pl.ds(pl.multiple_of(row * quarter + k * size, size), size)

    def py_copy(k):
        return remote(
            x_hbm.at[own_unit(k)], py.at[unit(k)], py_send.at[k], py_recv.at[k], col=y_mate
        )

    for k in range(UNITS):
        py_copy(k).start()
    for load in loads:
        load.wait()

    target = n // 4
    at = jnp.int32(0)
    for i in range(n):
        at = at + jnp.where(panel[i] == target, i, 0)
    root_here = at == col
    root_layer = at // 2 == z
    from_left = at // 2 <= z

    sums = jnp.zeros((blk, 128), F32)
    for j in range(0, width, 128):
        piece = x_ref[:, j:j + 128].astype(F32)
        sums = sums + piece * piece
    x_norm = jnp.sqrt(jnp.sum(sums.T, axis=0, keepdims=True) + EPS)
    x_inv = 1.0 / x_norm
    for i, term in enumerate(split3(inv_ref[...])):
        inv3[i] = term

    def block_kernel(a, a_f):
        a_norm = jnp.sqrt(jnp.sum(a_f * a_f, axis=1, keepdims=True) + EPS)
        u = dot_t(a, x_ref[...]) * (1.0 / a_norm) * x_inv
        return theta_of(u) * (a_norm * x_norm)

    def z_copy(buf, index, k, way, send, recv):
        return remote(
            buf.at[index], buf.at[index], send.at[way, k], recv.at[way, k],
            col=right if way == 0 else left,
        )

    def position(way):
        return z if way == 0 else nz - 1 - z

    def pass_on(buf, index, k, way, cand, send, recv):
        pos = position(way)

        @pl.when(pos == 0)
        def _():
            buf[index] = cand()

        @pl.when(pos > 0)
        def _():
            z_copy(buf, index, k, way, send, recv).wait_recv()
            buf[index] = lax.select(root_layer, cand(), buf[index])

        @pl.when(pos < nz - 1)
        def _():
            z_copy(buf, index, k, way, send, recv).start()

    def panel_slot(step):
        @pl.when(step < UNITS)
        def _():
            py_copy(step).wait_recv()
            own = x_ref[own_unit(step), :]
            py[unit(step), :] = lax.select(root_here, own, py[unit(step), :])

        for way, buf in enumerate((pr, plft)):
            k = step - HOP * position(way)

            @pl.when(jnp.logical_and(k >= 0, k < UNITS))
            def _():
                pass_on(buf, unit(k), k, way, lambda: py[unit(k), :], pz_send, pz_recv)

    def slots(first, last):
        @pl.loop(first, last)
        def _(step):
            panel_slot(step)

    def panel_group(g):
        sel = slice(g * quarter // GROUPS, (g + 1) * quarter // GROUPS)
        a = lax.select(from_left, pr[sel, :], plft[sel, :])
        kt[sel, :] = block_kernel(a, a.astype(F32))

    def work_rows():
        for d in range(1, n):
            slot = lax.rem(col + n - d, n)
            rows_copy(d, slot).wait_recv()
        for c in range(n):
            rows_all[c * per:(c + 1) * per, :] = rows_buf[c]
        a_f = rows_all[...]
        return block_kernel(a_f.astype(BF16), a_f)

    def wo_copy(d, slot):
        peer = lax.rem(row + d, nr)
        return remote(w_out.at[peer], wo.at[slot], wo_send.at[d], wo_recv.at[slot], row=peer)

    def wm_copy(d, slot):
        peer = lax.rem(row + d, nr)
        return remote(
            w_out.at[peer], wm.at[slot], wm_send.at[d], wm_recv.at[slot], row=peer, col=y_mate
        )

    def work_mid(a):
        low = product3(a[:, :half], [inv3[i, :half, :half] for i in range(3)], True)
        high = product3(a, [inv3[i, half:, :] for i in range(3)], True)
        return jnp.concatenate([low, high], axis=1)

    def work_w(mid):
        low = product3(mid, [inv3[i, :, :half] for i in range(3)], False)
        high = product3(mid[:, half:], [inv3[i, half:, half:] for i in range(3)], False)
        w = jnp.concatenate([low, high], axis=1)
        for j in range(nr):
            w_out[j] = w[:, j * quarter:(j + 1) * quarter]
        for d in range(nr):
            wm_copy(d, row).start()
        for d in range(1, nr):
            wo_copy(d, row).start()
        wo[row] = w_out[row]

    def work_exchange():
        for d in range(nr):
            slot = lax.rem(row + nr - d, nr)
            wm_copy(d, slot).wait_recv()
        for d in range(1, nr):
            slot = lax.rem(row + nr - d, nr)
            wo_copy(d, slot).wait_recv()
        for k in range(nr):
            wm[k] = lax.select(root_here, wo[k], wm[k])

    def w_hop(step):
        for way, buf in enumerate((wr, wl)):
            @pl.when(position(way) == step)
            def _():
                for k in range(nr):
                    pass_on(buf, k, k, way, lambda: wm[k], wz_send, wz_recv)

    last = UNITS + HOP * (nz - 1)
    middle = last - UNITS // 2
    slots(0, 2)
    k_rows = work_rows()
    slots(2, 4)
    mid = work_mid(k_rows)
    slots(4, 6)
    work_w(mid)
    slots(6, 8)
    work_exchange()
    w_hop(0)
    slots(8, middle - 2)
    w_hop(1)
    slots(middle - 2, middle)
    panel_group(0)
    w_hop(2)
    slots(middle, last)
    panel_group(1)

    @pl.loop(3, nz)
    def _(step):
        w_hop(step)

    def part_copy(d, slot):
        peer = lax.rem(row + d, nr)
        return remote(part.at[peer], part_in.at[slot], pt_send.at[d], pt_recv.at[slot], row=peer)

    w = jnp.concatenate([lax.select(from_left, wr[j], wl[j]) for j in range(nr)], axis=0)
    update = jnp.dot(w, kt[...], precision=lax.Precision.HIGHEST, preferred_element_type=F32)
    group = update.shape[0] // nr
    for j in range(nr):
        part[j] = update[j * group:(j + 1) * group]
    for d in range(1, nr):
        part_copy(d, row).start()
    total = part[row]
    for d in range(1, nr):
        slot = lax.rem(row + nr - d, nr)
        part_copy(d, slot).wait_recv()
        total = total + part_in[slot]
    trail = trail_ref[...]
    trail_ref[...] = lax.select(panel[col] > target, trail - total, trail)
    store = pltpu.make_async_copy(trail_ref, out_ref, in_sem.at[0])
    store.start()

    for d in range(1, n):
        rows_copy(d, col).wait_send()
    for k in range(UNITS):
        py_copy(k).wait_send()
    for d in range(nr):
        wm_copy(d, row).wait_send()
    for d in range(1, nr):
        wo_copy(d, row).wait_send()
        part_copy(d, row).wait_send()
    for way in (0, 1):
        @pl.when(position(way) < nz - 1)
        def _():
            for k in range(UNITS):
                z_copy((pr, plft)[way], unit(k), k, way, pz_send, pz_recv).wait_send()
            for k in range(nr):
                z_copy((wr, wl)[way], k, k, way, wz_send, wz_recv).wait_send()
    store.wait()


def on_device(n, nr, panel, centres_cols, centres_rows, diag_inverse, trailing):
    blk, width = centres_cols.shape
    quarter = blk // nr
    per = centres_rows.shape[0]
    group = per * n
    dma = pltpu.SemaphoreType.DMA
    vmem = pl.BlockSpec(memory_space=pltpu.VMEM)
    hbm = pl.BlockSpec(memory_space=pltpu.HBM)
    return pl.pallas_call(
        functools.partial(kernel, n, nr),
        out_shape=jax.ShapeDtypeStruct(trailing.shape, F32),
        in_specs=[hbm, hbm, vmem, hbm, hbm],
        out_specs=hbm,
        scratch_shapes=[
            pltpu.SMEM(panel.shape, jnp.int32),
            pltpu.VMEM(centres_cols.shape, BF16),
            pltpu.VMEM(diag_inverse.shape, F32),
            pltpu.VMEM(trailing.shape, F32),
            pltpu.VMEM((n, per, width), F32),
            pltpu.VMEM((group, width), F32),
            pltpu.VMEM((3, blk, blk), BF16),
            pltpu.VMEM((quarter, width), BF16),
            pltpu.VMEM((quarter, width), BF16),
            pltpu.VMEM((quarter, width), BF16),
            pltpu.VMEM((nr, group, quarter), F32),
            pltpu.VMEM((nr, group, quarter), F32),
            pltpu.VMEM((nr, group, quarter), F32),
            pltpu.VMEM((nr, group, quarter), F32),
            pltpu.VMEM((nr, group, quarter), F32),
            pltpu.VMEM((quarter, blk), F32),
            pltpu.VMEM((nr, group, blk), F32),
            pltpu.VMEM((nr, group, blk), F32),
            dma((4,)),
            dma((n,)), dma((n,)),
            dma((UNITS,)), dma((UNITS,)),
            dma((2, UNITS)), dma((2, UNITS)),
            dma((nr,)), dma((nr,)),
            dma((nr,)), dma((nr,)),
            dma((2, nr)), dma((2, nr)),
            dma((nr,)), dma((nr,)),
        ],
        compiler_params=pltpu.CompilerParams(
            collective_id=0, has_side_effects=True, vmem_limit_bytes=VMEM_BYTES
        ),
    )(panel, centres_cols, centres_rows, diag_inverse, trailing)


def solution(mesh):
    return jax.shard_map(
        functools.partial(on_device, mesh.shape["col"], mesh.shape["row"]),
        mesh=mesh,
        in_specs=(P(), P("col", None), P(("row", "col"), None), P("col", None), P("row", "col")),
        out_specs=P("row", "col"),
        check_vma=False,
    )
```

```python
import functools
import math

import jax
import jax.numpy as jnp
from jax import lax
from jax.experimental import pallas as pl
from jax.experimental.pallas import tpu as pltpu
from jax.sharding import PartitionSpec as P

LAYERS = 3
EPS = 1e-06
UNITS = 8
GROUPS = 2
HOP = 3
VMEM_BYTES = 63 * 2**20
MESH = pl.DeviceIdType.MESH
F32 = jnp.float32
BF16 = jnp.bfloat16
ACOS = tuple(
    v / math.pi
    for v in (
        1.5707963050, -0.2145988016, 0.0889789874, -0.0501743046,
        0.0308918810, -0.0170881256, 0.0066700901, -0.0012624911,
    )
)


def root(y):
    y = jnp.maximum(y, 1e-30)
    return y * lax.rsqrt(y)


def theta_of(u):
    rho = jnp.clip(u, -1.0, 1.0)
    theta = rho
    for layer in range(LAYERS):
        size = jnp.abs(rho) if layer == 0 else rho
        poly = jnp.full_like(size, ACOS[-1])
        for coef in ACOS[-2::-1]:
            poly = poly * size + coef
        low = root(1.0 - size)
        angle = low * poly
        sine = low * root(1.0 + size)
        if layer == 0:
            zero_order = jnp.where(rho < 0.0, angle, 1.0 - angle)
        else:
            zero_order = 1.0 - angle
        rho_next = sine * (1.0 / math.pi) + zero_order * rho
        theta = theta * zero_order + rho_next
        rho = rho_next
    return theta


def dot_t(a, b, precision=None):
    return lax.dot_general(
        a, b, (((1,), (1,)), ((), ())), precision=precision, preferred_element_type=F32
    )


def split3(a):
    hi = a.astype(BF16)
    rest = a - hi.astype(F32)
    mid = rest.astype(BF16)
    return hi, mid, (rest - mid.astype(F32)).astype(BF16)


def product3(a, weights, transposed):
    m = a.shape[0]
    terms = jnp.concatenate(split3(a), axis=0)
    dims = (((1,), (1 if transposed else 0,)), ((), ()))

    def mul(count, w):
        return lax.dot_general(terms[:count * m], w, dims, preferred_element_type=F32)

    p, q, t = mul(3, weights[0]), mul(2, weights[1]), mul(1, weights[2])
    small = t + q[m:] + p[2 * m:]
    return (small + (q[:m] + p[m:2 * m])) + p[:m]


def kernel(
    n, nr, panel_hbm, x_hbm, rows_ref, inv_hbm, trail_hbm, out_ref,
    panel, x_ref, inv_ref, trail_ref,
    rows_buf, rows_all, inv3, py, pr, plft, w_out, wo, wm, wr, wl, kt, part, part_in,
    in_sem, rows_send, rows_recv, py_send, py_recv, pz_send, pz_recv,
    wo_send, wo_recv, wm_send, wm_recv, wz_send, wz_recv, pt_send, pt_recv,
):
    col = lax.axis_index("col")
    row = lax.axis_index("row")
    nz = n // 2
    z, y = col // 2, col % 2
    y_mate = z * 2 + 1 - y
    right, left = lax.rem(col + 2, n), lax.rem(col + n - 2, n)
    blk, width = x_ref.shape
    half = blk // 2
    quarter = blk // nr
    size = quarter // UNITS
    per = rows_ref.shape[0]

    barrier = pltpu.get_barrier_semaphore()

    def greet(**where):
        pl.semaphore_signal(barrier, inc=1, device_id=where, device_id_type=MESH)

    for d in range(1, n):
        greet(col=lax.rem(col + d, n))
    for d in range(1, nr):
        greet(row=lax.rem(row + d, nr))
        greet(row=lax.rem(row + d, nr), col=y_mate)
    loads = [
        pltpu.make_async_copy(src, dst, in_sem.at[i])
        for i, (src, dst) in enumerate(
            ((panel_hbm, panel), (x_hbm, x_ref), (inv_hbm, inv_ref), (trail_hbm, trail_ref))
        )
    ]
    for load in loads:
        load.start()
    rows_buf[col] = rows_ref[...].astype(F32)
    pl.semaphore_wait(barrier, n - 1 + 2 * (nr - 1))

    def remote(src, dst, send, recv, **where):
        return pltpu.make_async_remote_copy(
            src_ref=src, dst_ref=dst, send_sem=send, recv_sem=recv,
            device_id=where, device_id_type=MESH,
        )

    def rows_copy(d, slot):
        return remote(
            rows_buf.at[slot], rows_buf.at[slot], rows_send.at[d], rows_recv.at[slot],
            col=lax.rem(col + d, n),
        )

    for d in range(1, n):
        rows_copy(d, col).start()

    def unit(k):
        return pl.ds(pl.multiple_of(k * size, size), size)

    def own_unit(k):
        return pl.ds(pl.multiple_of(row * quarter + k * size, size), size)

    def py_copy(k):
        return remote(
            x_hbm.at[own_unit(k)], py.at[unit(k)], py_send.at[k], py_recv.at[k], col=y_mate
        )

    for k in range(UNITS):
        py_copy(k).start()
    for load in loads:
        load.wait()

    target = n // 4
    at = jnp.int32(0)
    for i in range(n):
        at = at + jnp.where(panel[i] == target, i, 0)
    root_here = at == col
    root_layer = at // 2 == z
    from_left = at // 2 <= z

    sums = jnp.zeros((blk, 128), F32)
    for j in range(0, width, 128):
        piece = x_ref[:, j:j + 128].astype(F32)
        sums = sums + piece * piece
    x_norm = jnp.sqrt(jnp.sum(sums.T, axis=0, keepdims=True) + EPS)
    x_inv = 1.0 / x_norm
    for i, term in enumerate(split3(inv_ref[...])):
        inv3[i] = term

    def block_kernel(a, a_f):
        a_norm = jnp.sqrt(jnp.sum(a_f * a_f, axis=1, keepdims=True) + EPS)
        u = dot_t(a, x_ref[...]) * (1.0 / a_norm) * x_inv
        return theta_of(u) * (a_norm * x_norm)

    def z_copy(buf, index, k, way, send, recv):
        return remote(
            buf.at[index], buf.at[index], send.at[way, k], recv.at[way, k],
            col=right if way == 0 else left,
        )

    def position(way):
        return z if way == 0 else nz - 1 - z

    def pass_on(buf, index, k, way, cand, send, recv):
        pos = position(way)

        @pl.when(pos == 0)
        def _():
            buf[index] = cand()

        @pl.when(pos > 0)
        def _():
            z_copy(buf, index, k, way, send, recv).wait_recv()
            buf[index] = lax.select(root_layer, cand(), buf[index])

        @pl.when(pos < nz - 1)
        def _():
            z_copy(buf, index, k, way, send, recv).start()

    def panel_slot(step):
        @pl.when(step < UNITS)
        def _():
            py_copy(step).wait_recv()
            own = x_ref[own_unit(step), :]
            py[unit(step), :] = lax.select(root_here, own, py[unit(step), :])

        for way, buf in enumerate((pr, plft)):
            k = step - HOP * position(way)

            @pl.when(jnp.logical_and(k >= 0, k < UNITS))
            def _():
                pass_on(buf, unit(k), k, way, lambda: py[unit(k), :], pz_send, pz_recv)

    def slots(first, last):
        @pl.loop(first, last)
        def _(step):
            panel_slot(step)

    def panel_group(g):
        sel = slice(g * quarter // GROUPS, (g + 1) * quarter // GROUPS)
        a = lax.select(from_left, pr[sel, :], plft[sel, :])
        kt[sel, :] = block_kernel(a, a.astype(F32))

    def work_rows():
        for d in range(1, n):
            slot = lax.rem(col + n - d, n)
            rows_copy(d, slot).wait_recv()
        for c in range(n):
            rows_all[c * per:(c + 1) * per, :] = rows_buf[c]
        a_f = rows_all[...]
        return block_kernel(a_f.astype(BF16), a_f)

    def wo_copy(d, slot):
        peer = lax.rem(row + d, nr)
        return remote(w_out.at[peer], wo.at[slot], wo_send.at[d], wo_recv.at[slot], row=peer)

    def wm_copy(d, slot):
        peer = lax.rem(row + d, nr)
        return remote(
            w_out.at[peer], wm.at[slot], wm_send.at[d], wm_recv.at[slot], row=peer, col=y_mate
        )

    def work_mid(a):
        low = product3(a[:, :half], [inv3[i, :half, :half] for i in range(3)], True)
        high = product3(a, [inv3[i, half:, :] for i in range(3)], True)
        return jnp.concatenate([low, high], axis=1)

    def work_w(mid):
        low = product3(mid, [inv3[i, :, :half] for i in range(3)], False)
        high = product3(mid[:, half:], [inv3[i, half:, half:] for i in range(3)], False)
        w = jnp.concatenate([low, high], axis=1)
        for j in range(nr):
            w_out[j] = w[:, j * quarter:(j + 1) * quarter]
        for d in range(nr):
            wm_copy(d, row).start()
        for d in range(1, nr):
            wo_copy(d, row).start()
        wo[row] = w_out[row]

    def work_exchange():
        for d in range(nr):
            slot = lax.rem(row + nr - d, nr)
            wm_copy(d, slot).wait_recv()
        for d in range(1, nr):
            slot = lax.rem(row + nr - d, nr)
            wo_copy(d, slot).wait_recv()
        for k in range(nr):
            wm[k] = lax.select(root_here, wo[k], wm[k])

    def w_hop(step):
        for way, buf in enumerate((wr, wl)):
            @pl.when(position(way) == step)
            def _():
                for k in range(nr):
                    pass_on(buf, k, k, way, lambda: wm[k], wz_send, wz_recv)

    last = UNITS + HOP * (nz - 1)
    middle = last - UNITS // 2
    slots(0, 2)
    k_rows = work_rows()
    slots(2, 4)
    mid = work_mid(k_rows)
    slots(4, 6)
    work_w(mid)
    slots(6, 8)
    work_exchange()
    w_hop(0)
    slots(8, middle - 2)
    w_hop(1)
    slots(middle - 2, middle)
    panel_group(0)
    w_hop(2)
    slots(middle, last)
    panel_group(1)

    @pl.loop(3, nz)
    def _(step):
        w_hop(step)

    def part_copy(d, slot):
        peer = lax.rem(row + d, nr)
        return remote(part.at[peer], part_in.at[slot], pt_send.at[d], pt_recv.at[slot], row=peer)

    w = jnp.concatenate([lax.select(from_left, wr[j], wl[j]) for j in range(nr)], axis=0)
    update = jnp.dot(w, kt[...], precision=lax.Precision.HIGHEST, preferred_element_type=F32)
    group = update.shape[0] // nr
    for j in range(nr):
        part[j] = update[j * group:(j + 1) * group]
    for d in range(1, nr):
        part_copy(d, row).start()
    total = part[row]
    for d in range(1, nr):
        slot = lax.rem(row + nr - d, nr)
        part_copy(d, slot).wait_recv()
        total = total + part_in[slot]
    trail = trail_ref[...]
    trail_ref[...] = lax.select(panel[col] > target, trail - total, trail)
    store = pltpu.make_async_copy(trail_ref, out_ref, in_sem.at[0])
    store.start()

    for d in range(1, n):
        rows_copy(d, col).wait_send()
    for k in range(UNITS):
        py_copy(k).wait_send()
    for d in range(nr):
        wm_copy(d, row).wait_send()
    for d in range(1, nr):
        wo_copy(d, row).wait_send()
        part_copy(d, row).wait_send()
    for way in (0, 1):
        @pl.when(position(way) < nz - 1)
        def _():
            for k in range(UNITS):
                z_copy((pr, plft)[way], unit(k), k, way, pz_send, pz_recv).wait_send()
            for k in range(nr):
                z_copy((wr, wl)[way], k, k, way, wz_send, wz_recv).wait_send()
    store.wait()


def rooted(
    root, n, nr, panel_hbm, x_hbm, rows_ref, inv_hbm, trail_hbm, out_ref,
    panel, x_ref, inv_ref, trail_ref, rows_buf, rows_all, inv3, px, w_out, w_in, kt, part, part_in,
    in_sem, rows_send, rows_recv, px_send, px_recv, w_send, w_recv, pt_send, pt_recv,
):
    col = lax.axis_index("col")
    row = lax.axis_index("row")
    nz = n // 2
    z, root_z = col // 2, root // 2
    mate = root + 1 - 2 * (root % 2)
    blk, width = x_ref.shape
    half = blk // 2
    quarter = blk // nr
    size = quarter // UNITS
    per = rows_ref.shape[0]
    others = [c for c in range(n) if c != root]

    barrier = pltpu.get_barrier_semaphore()

    def greet(**where):
        pl.semaphore_signal(barrier, inc=1, device_id=where, device_id_type=MESH)

    def remote(src, dst, send, recv, **where):
        return pltpu.make_async_remote_copy(
            src_ref=src, dst_ref=dst, send_sem=send, recv_sem=recv,
            device_id=where, device_id_type=MESH,
        )

    loads = [
        pltpu.make_async_copy(src, dst, in_sem.at[i])
        for i, (src, dst) in enumerate(
            ((panel_hbm, panel), (x_hbm, x_ref), (trail_hbm, trail_ref), (inv_hbm, inv_ref))
        )
    ]

    for d in range(1, n):
        greet(col=lax.rem(col + d, n))
    for d in range(1, nr):
        greet(row=lax.rem(row + d, nr))
    for load in loads[:3]:
        load.start()

    def unit(k):
        return pl.ds(pl.multiple_of(k * size, size), size)

    def block_norm():
        sums = jnp.zeros((blk, 128), F32)
        for j in range(0, width, 128):
            piece = x_ref[:, j:j + 128].astype(F32)
            sums = sums + piece * piece
        return jnp.sqrt(jnp.sum(sums.T, axis=0, keepdims=True) + EPS)

    def block_kernel(a, a_f, x_norm):
        a_norm = jnp.sqrt(jnp.sum(a_f * a_f, axis=1, keepdims=True) + EPS)
        u = dot_t(a, x_ref[...]) * (1.0 / a_norm) * (1.0 / x_norm)
        return theta_of(u) * (a_norm * x_norm)

    def rows_copy(slot):
        return remote(
            rows_buf.at[slot], rows_buf.at[slot], rows_send.at[0], rows_recv.at[slot], col=root
        )

    def w_copy(d, c, slot):
        peer = lax.rem(row + d, nr)
        return remote(
            w_out.at[peer], w_in.at[slot], w_send.at[d, c], w_recv.at[slot], row=peer, col=c
        )

    def part_copy(d, slot):
        peer = lax.rem(row + d, nr)
        return remote(part.at[peer], part_in.at[slot], pt_send.at[d], pt_recv.at[slot], row=peer)

    rows_buf[col] = rows_ref[...].astype(F32)

    @pl.when(col == root)
    def _():
        loads[3].start()
        for d in range(1, nr):
            for c in others:
                greet(row=lax.rem(row + d, nr), col=c)
        pl.semaphore_wait(barrier, nr * n - 1)

        def send(k, way, to):
            src = x_hbm.at[pl.ds(pl.multiple_of(row * quarter + k * size, size), size)]
            return remote(src, px.at[unit(k)], px_send.at[way, k], px_recv.at[k], col=to)

        targets = [(0, mate)]
        if root_z < nz - 1:
            targets.append((1, root + 2))
        if root_z > 0:
            targets.append((2, root - 2))
        for k in range(UNITS):
            for way, to in targets:
                send(k, way, to).start()
        for load in loads:
            load.wait()
        store = pltpu.make_async_copy(trail_ref, out_ref, in_sem.at[0])
        store.start()
        x_norm = block_norm()
        for i, term in enumerate(split3(inv_ref[...])):
            inv3[i] = term
        for c in others:
            rows_copy(c).wait_recv()
        for c in range(n):
            rows_all[c * per:(c + 1) * per, :] = rows_buf[c]
        a_f = rows_all[...]
        a = block_kernel(a_f.astype(BF16), a_f, x_norm)
        low = product3(a[:, :half], [inv3[i, :half, :half] for i in range(3)], True)
        high = product3(a, [inv3[i, half:, :] for i in range(3)], True)
        mid = jnp.concatenate([low, high], axis=1)
        low = product3(mid, [inv3[i, :, :half] for i in range(3)], False)
        high = product3(mid[:, half:], [inv3[i, half:, half:] for i in range(3)], False)
        w = jnp.concatenate([low, high], axis=1)
        for j in range(nr):
            w_out[j] = w[:, j * quarter:(j + 1) * quarter]
        far = sorted(others, key=lambda c: -abs(c // 2 - root_z))
        for c in far:
            for d in range(nr):
                w_copy(d, c, row).start()
        for c in others:
            for d in range(nr):
                w_copy(d, c, row).wait_send()
        for k in range(UNITS):
            for way, to in targets:
                send(k, way, to).wait_send()
        store.wait()

    @pl.when(col != root)
    def _():
        for d in range(1, nr):
            greet(row=lax.rem(row + d, nr), col=root)
        pl.semaphore_wait(barrier, n - 1 + 2 * (nr - 1))
        rows_copy(col).start()
        for load in loads[:3]:
            load.wait()
        x_norm = block_norm()
        up = jnp.logical_and(z >= root_z, z < nz - 1)
        down = jnp.logical_and(z <= root_z, z > 0)
        leaf = jnp.logical_not(jnp.logical_or(up, down))

        def pass_copy(k, way):
            to = lax.rem(col + (2 if way == 1 else n - 2), n)
            return remote(
                px.at[unit(k)], px.at[unit(k)], px_send.at[way, k], px_recv.at[k], col=to
            )

        def relay(first, last):
            for k in range(first, last):
                pass_copy(k, 1).wait_recv()

                @pl.when(up)
                def _():
                    pass_copy(k, 1).start()

                @pl.when(down)
                def _():
                    pass_copy(k, 2).start()

        def panel_group(g):
            sel = slice(g * quarter // 2, (g + 1) * quarter // 2)
            a = px[sel, :]
            kt[sel, :] = block_kernel(a, a.astype(F32), x_norm)

        relay(0, UNITS // 2)

        @pl.when(leaf)
        def _():
            panel_group(0)

        relay(UNITS // 2, UNITS)

        @pl.when(jnp.logical_not(leaf))
        def _():
            panel_group(0)

        panel_group(1)
        for d in range(nr):
            slot = lax.rem(row + nr - d, nr)
            w_copy(d, col, slot).wait_recv()
        w = jnp.concatenate([w_in[j] for j in range(nr)], axis=0)
        update = jnp.dot(w, kt[...], precision=lax.Precision.HIGHEST, preferred_element_type=F32)
        group = update.shape[0] // nr
        for j in range(nr):
            part[j] = update[j * group:(j + 1) * group]
        for d in range(1, nr):
            part_copy(d, row).start()
        total = part[row]
        for d in range(1, nr):
            slot = lax.rem(row + nr - d, nr)
            part_copy(d, slot).wait_recv()
            total = total + part_in[slot]
        trail = trail_ref[...]
        trail_ref[...] = lax.select(panel[col] > n // 4, trail - total, trail)
        store = pltpu.make_async_copy(trail_ref, out_ref, in_sem.at[0])
        store.start()
        rows_copy(col).wait_send()
        for d in range(1, nr):
            part_copy(d, row).wait_send()

        @pl.when(up)
        def _():
            for k in range(UNITS):
                pass_copy(k, 1).wait_send()

        @pl.when(down)
        def _():
            for k in range(UNITS):
                pass_copy(k, 2).wait_send()

        store.wait()


def rooted_call(root, n, nr, panel, centres_cols, centres_rows, diag_inverse, trailing):
    blk, width = centres_cols.shape
    quarter = blk // nr
    per = centres_rows.shape[0]
    group = per * n
    dma = pltpu.SemaphoreType.DMA
    hbm = pl.BlockSpec(memory_space=pltpu.HBM)
    return pl.pallas_call(
        functools.partial(rooted, root, n, nr),
        out_shape=jax.ShapeDtypeStruct(trailing.shape, F32),
        in_specs=[hbm, hbm, pl.BlockSpec(memory_space=pltpu.VMEM), hbm, hbm],
        out_specs=hbm,
        scratch_shapes=[
            pltpu.SMEM(panel.shape, jnp.int32),
            pltpu.VMEM(centres_cols.shape, BF16),
            pltpu.VMEM(diag_inverse.shape, F32),
            pltpu.VMEM(trailing.shape, F32),
            pltpu.VMEM((n, per, width), F32),
            pltpu.VMEM((group, width), F32),
            pltpu.VMEM((3, blk, blk), BF16),
            pltpu.VMEM((quarter, width), BF16),
            pltpu.VMEM((nr, group, quarter), F32),
            pltpu.VMEM((nr, group, quarter), F32),
            pltpu.VMEM((quarter, blk), F32),
            pltpu.VMEM((nr, group, blk), F32),
            pltpu.VMEM((nr, group, blk), F32),
            dma((4,)),
            dma((1,)), dma((n,)),
            dma((3, UNITS)), dma((UNITS,)),
            dma((nr, n)), dma((nr,)),
            dma((nr,)), dma((nr,)),
        ],
        compiler_params=pltpu.CompilerParams(
            collective_id=root, has_side_effects=True, vmem_limit_bytes=VMEM_BYTES
        ),
    )(panel, centres_cols, centres_rows, diag_inverse, trailing)


def on_device(n, nr, panel, centres_cols, centres_rows, diag_inverse, trailing):
    if n <= 8:
        at = jnp.sum(jnp.where(panel == n // 4, jnp.arange(n, dtype=jnp.int32), 0))
        branches = [functools.partial(rooted_call, root, n, nr) for root in range(n)]
        return lax.switch(
            at, branches, panel, centres_cols, centres_rows, diag_inverse, trailing
        )
    blk, width = centres_cols.shape
    quarter = blk // nr
    per = centres_rows.shape[0]
    group = per * n
    dma = pltpu.SemaphoreType.DMA
    vmem = pl.BlockSpec(memory_space=pltpu.VMEM)
    hbm = pl.BlockSpec(memory_space=pltpu.HBM)
    return pl.pallas_call(
        functools.partial(kernel, n, nr),
        out_shape=jax.ShapeDtypeStruct(trailing.shape, F32),
        in_specs=[hbm, hbm, vmem, hbm, hbm],
        out_specs=hbm,
        scratch_shapes=[
            pltpu.SMEM(panel.shape, jnp.int32),
            pltpu.VMEM(centres_cols.shape, BF16),
            pltpu.VMEM(diag_inverse.shape, F32),
            pltpu.VMEM(trailing.shape, F32),
            pltpu.VMEM((n, per, width), F32),
            pltpu.VMEM((group, width), F32),
            pltpu.VMEM((3, blk, blk), BF16),
            pltpu.VMEM((quarter, width), BF16),
            pltpu.VMEM((quarter, width), BF16),
            pltpu.VMEM((quarter, width), BF16),
            pltpu.VMEM((nr, group, quarter), F32),
            pltpu.VMEM((nr, group, quarter), F32),
            pltpu.VMEM((nr, group, quarter), F32),
            pltpu.VMEM((nr, group, quarter), F32),
            pltpu.VMEM((nr, group, quarter), F32),
            pltpu.VMEM((quarter, blk), F32),
            pltpu.VMEM((nr, group, blk), F32),
            pltpu.VMEM((nr, group, blk), F32),
            dma((4,)),
            dma((n,)), dma((n,)),
            dma((UNITS,)), dma((UNITS,)),
            dma((2, UNITS)), dma((2, UNITS)),
            dma((nr,)), dma((nr,)),
            dma((nr,)), dma((nr,)),
            dma((2, nr)), dma((2, nr)),
            dma((nr,)), dma((nr,)),
        ],
        compiler_params=pltpu.CompilerParams(
            collective_id=0, has_side_effects=True, vmem_limit_bytes=VMEM_BYTES
        ),
    )(panel, centres_cols, centres_rows, diag_inverse, trailing)


def solution(mesh):
    return jax.shard_map(
        functools.partial(on_device, mesh.shape["col"], mesh.shape["row"]),
        mesh=mesh,
        in_specs=(P(), P("col", None), P(("row", "col"), None), P("col", None), P("row", "col")),
        out_specs=P("row", "col"),
        check_vma=False,
    )
```

```python
import functools
import math

import jax
import jax.numpy as jnp
from jax import lax
from jax.experimental import pallas as pl
from jax.experimental.pallas import tpu as pltpu
from jax.sharding import PartitionSpec as P

LAYERS = 3
EPS = 1e-06
UNITS = 4
HOP = 3
VMEM_BYTES = 63 * 2**20
MESH = pl.DeviceIdType.MESH
F32 = jnp.float32
BF16 = jnp.bfloat16
ACOS = tuple(
    v / math.pi
    for v in (
        1.5707963050, -0.2145988016, 0.0889789874, -0.0501743046,
        0.0308918810, -0.0170881256, 0.0066700901, -0.0012624911,
    )
)


def root(y):
    y = jnp.maximum(y, 1e-30)
    return y * lax.rsqrt(y)


def theta_of(u):
    rho = jnp.clip(u, -1.0, 1.0)
    theta = rho
    for layer in range(LAYERS):
        size = jnp.abs(rho) if layer == 0 else rho
        poly = jnp.full_like(size, ACOS[-1])
        for coef in ACOS[-2::-1]:
            poly = poly * size + coef
        low = root(1.0 - size)
        angle = low * poly
        sine = low * root(1.0 + size)
        if layer == 0:
            zero_order = jnp.where(rho < 0.0, angle, 1.0 - angle)
        else:
            zero_order = 1.0 - angle
        rho_next = sine * (1.0 / math.pi) + zero_order * rho
        theta = theta * zero_order + rho_next
        rho = rho_next
    return theta


def dot_t(a, b, precision=None):
    return lax.dot_general(
        a, b, (((1,), (1,)), ((), ())), precision=precision, preferred_element_type=F32
    )


def split3(a):
    hi = a.astype(BF16)
    rest = a - hi.astype(F32)
    mid = rest.astype(BF16)
    return hi, mid, (rest - mid.astype(F32)).astype(BF16)


def product3(a, weights, transposed):
    m = a.shape[0]
    terms = jnp.concatenate(split3(a), axis=0)
    dims = (((1,), (1 if transposed else 0,)), ((), ()))

    def mul(count, w):
        return lax.dot_general(terms[:count * m], w, dims, preferred_element_type=F32)

    p, q, t = mul(3, weights[0]), mul(2, weights[1]), mul(1, weights[2])
    small = t + q[m:] + p[2 * m:]
    return (small + (q[:m] + p[m:2 * m])) + p[:m]


def kernel(
    n, nr, panel_hbm, x_hbm, rows_ref, inv_hbm, trail_hbm, out_ref,
    panel, x_ref, inv_ref, trail_ref,
    rows_buf, rows_all, inv3, py, pr, plft, done, across, w_out, wo, wm, wr, wl, kt, part, part_in,
    in_sem, rows_send, rows_recv, py_send, py_recv, pz_send, pz_recv, cx_send, cx_recv,
    wo_send, wo_recv, wm_send, wm_recv, wz_send, wz_recv, pt_send, pt_recv,
):
    col = lax.axis_index("col")
    row = lax.axis_index("row")
    nz = n // 2
    z, y = col // 2, col % 2
    y_mate = z * 2 + 1 - y
    right, left = lax.rem(col + 2, n), lax.rem(col + n - 2, n)
    blk, width = x_ref.shape
    half = blk // 2
    quarter = blk // nr
    share = quarter // 2
    size = share // UNITS
    per = rows_ref.shape[0]

    barrier = pltpu.get_barrier_semaphore()

    def greet(**where):
        pl.semaphore_signal(barrier, inc=1, device_id=where, device_id_type=MESH)

    for d in range(1, n):
        greet(col=lax.rem(col + d, n))
    for d in range(1, nr):
        greet(row=lax.rem(row + d, nr))
        greet(row=lax.rem(row + d, nr), col=y_mate)
    loads = [
        pltpu.make_async_copy(src, dst, in_sem.at[i])
        for i, (src, dst) in enumerate(
            ((panel_hbm, panel), (x_hbm, x_ref), (inv_hbm, inv_ref), (trail_hbm, trail_ref))
        )
    ]
    for load in loads:
        load.start()
    rows_buf[col] = rows_ref[...].astype(F32)
    pl.semaphore_wait(barrier, n - 1 + 2 * (nr - 1))

    def remote(src, dst, send, recv, **where):
        return pltpu.make_async_remote_copy(
            src_ref=src, dst_ref=dst, send_sem=send, recv_sem=recv,
            device_id=where, device_id_type=MESH,
        )

    def rows_copy(d, slot):
        return remote(
            rows_buf.at[slot], rows_buf.at[slot], rows_send.at[d], rows_recv.at[slot],
            col=lax.rem(col + d, n),
        )

    for d in range(1, n):
        rows_copy(d, col).start()

    def unit(k):
        return pl.ds(pl.multiple_of(k * size, size), size)

    def own_unit(side, k):
        return pl.ds(pl.multiple_of(row * quarter + side * share + k * size, size), size)

    def py_copy(k):
        return remote(
            x_hbm.at[own_unit(1 - y, k)], py.at[unit(k)], py_send.at[k], py_recv.at[k], col=y_mate
        )

    def cx_copy(k):
        return remote(
            done.at[unit(k)], across.at[unit(k)], cx_send.at[k], cx_recv.at[k], col=y_mate
        )

    for k in range(UNITS):
        py_copy(k).start()
    for load in loads:
        load.wait()

    target = n // 4
    at = jnp.int32(0)
    for i in range(n):
        at = at + jnp.where(panel[i] == target, i, 0)
    root_here = at == col
    root_layer = at // 2 == z
    from_left = at // 2 <= z

    sums = jnp.zeros((blk, 128), F32)
    for j in range(0, width, 128):
        piece = x_ref[:, j:j + 128].astype(F32)
        sums = sums + piece * piece
    x_norm = jnp.sqrt(jnp.sum(sums.T, axis=0, keepdims=True) + EPS)
    x_inv = 1.0 / x_norm
    for i, term in enumerate(split3(inv_ref[...])):
        inv3[i] = term

    def block_kernel(a, a_f):
        a_norm = jnp.sqrt(jnp.sum(a_f * a_f, axis=1, keepdims=True) + EPS)
        u = dot_t(a, x_ref[...]) * (1.0 / a_norm) * x_inv
        return theta_of(u) * (a_norm * x_norm)

    def z_copy(buf, index, k, way, send, recv):
        return remote(
            buf.at[index], buf.at[index], send.at[way, k], recv.at[way, k],
            col=right if way == 0 else left,
        )

    def position(way):
        return z if way == 0 else nz - 1 - z

    def pass_on(buf, index, k, way, cand, send, recv):
        pos = position(way)

        @pl.when(pos == 0)
        def _():
            buf[index] = cand()

        @pl.when(pos > 0)
        def _():
            z_copy(buf, index, k, way, send, recv).wait_recv()
            buf[index] = lax.select(root_layer, cand(), buf[index])

        @pl.when(pos < nz - 1)
        def _():
            z_copy(buf, index, k, way, send, recv).start()

    def panel_slot(step):
        @pl.when(step < UNITS)
        def _():
            py_copy(step).wait_recv()
            own = x_ref[own_unit(y, step), :]
            py[unit(step), :] = lax.select(root_here, own, py[unit(step), :])

        for way, buf in enumerate((pr, plft)):
            k = step - HOP * position(way)

            @pl.when(jnp.logical_and(k >= 0, k < UNITS))
            def _():
                pass_on(buf, unit(k), k, way, lambda: py[unit(k), :], pz_send, pz_recv)

        k_done = step - HOP * (nz - 1)

        @pl.when(k_done >= 0)
        def _():
            sel = unit(k_done)
            done[sel, :] = lax.select(from_left, pr[sel, :], plft[sel, :])
            cx_copy(k_done).start()

    def slots(first, last):
        @pl.loop(first, last)
        def _(step):
            panel_slot(step)

    def panel_half(side, a):
        kt[pl.ds(pl.multiple_of(side * share, share), share), :] = block_kernel(a, a.astype(F32))

    def work_rows():
        for d in range(1, n):
            slot = lax.rem(col + n - d, n)
            rows_copy(d, slot).wait_recv()
        for c in range(n):
            rows_all[c * per:(c + 1) * per, :] = rows_buf[c]
        a_f = rows_all[...]
        return block_kernel(a_f.astype(BF16), a_f)

    def wo_copy(d, slot):
        peer = lax.rem(row + d, nr)
        return remote(w_out.at[peer], wo.at[slot], wo_send.at[d], wo_recv.at[slot], row=peer)

    def wm_copy(d, slot):
        peer = lax.rem(row + d, nr)
        return remote(
            w_out.at[peer], wm.at[slot], wm_send.at[d], wm_recv.at[slot], row=peer, col=y_mate
        )

    def work_mid(a):
        low = product3(a[:, :half], [inv3[i, :half, :half] for i in range(3)], True)
        high = product3(a, [inv3[i, half:, :] for i in range(3)], True)
        return jnp.concatenate([low, high], axis=1)

    def work_w(mid):
        low = product3(mid, [inv3[i, :, :half] for i in range(3)], False)
        high = product3(mid[:, half:], [inv3[i, half:, half:] for i in range(3)], False)
        w = jnp.concatenate([low, high], axis=1)
        for j in range(nr):
            w_out[j] = w[:, j * quarter:(j + 1) * quarter]
        for d in range(nr):
            wm_copy(d, row).start()
        for d in range(1, nr):
            wo_copy(d, row).start()
        wo[row] = w_out[row]

    def work_exchange():
        for d in range(nr):
            slot = lax.rem(row + nr - d, nr)
            wm_copy(d, slot).wait_recv()
        for d in range(1, nr):
            slot = lax.rem(row + nr - d, nr)
            wo_copy(d, slot).wait_recv()
        for k in range(nr):
            wm[k] = lax.select(root_here, wo[k], wm[k])

    def w_hop(step):
        for way, buf in enumerate((wr, wl)):
            @pl.when(position(way) == step)
            def _():
                for k in range(nr):
                    pass_on(buf, k, k, way, lambda: wm[k], wz_send, wz_recv)

    last = UNITS + HOP * (nz - 1)
    slots(0, 2)
    k_rows = work_rows()
    slots(2, 4)
    mid = work_mid(k_rows)
    slots(4, 6)
    work_w(mid)
    slots(6, 8)
    work_exchange()
    w_hop(0)
    slots(8, last - 3)
    w_hop(1)
    slots(last - 3, last - 1)
    w_hop(2)
    slots(last - 1, last)
    panel_half(y, done[...])
    for k in range(UNITS):
        cx_copy(k).wait_recv()
    panel_half(1 - y, across[...])

    @pl.loop(3, nz)
    def _(step):
        w_hop(step)

    def part_copy(d, slot):
        peer = lax.rem(row + d, nr)
        return remote(part.at[peer], part_in.at[slot], pt_send.at[d], pt_recv.at[slot], row=peer)

    w = jnp.concatenate([lax.select(from_left, wr[j], wl[j]) for j in range(nr)], axis=0)
    update = jnp.dot(w, kt[...], precision=lax.Precision.HIGHEST, preferred_element_type=F32)
    group = update.shape[0] // nr
    for j in range(nr):
        part[j] = update[j * group:(j + 1) * group]
    for d in range(1, nr):
        part_copy(d, row).start()
    total = part[row]
    for d in range(1, nr):
        slot = lax.rem(row + nr - d, nr)
        part_copy(d, slot).wait_recv()
        total = total + part_in[slot]
    trail = trail_ref[...]
    trail_ref[...] = lax.select(panel[col] > target, trail - total, trail)
    store = pltpu.make_async_copy(trail_ref, out_ref, in_sem.at[0])
    store.start()

    for d in range(1, n):
        rows_copy(d, col).wait_send()
    for k in range(UNITS):
        py_copy(k).wait_send()
        cx_copy(k).wait_send()
    for d in range(nr):
        wm_copy(d, row).wait_send()
    for d in range(1, nr):
        wo_copy(d, row).wait_send()
        part_copy(d, row).wait_send()
    for way in (0, 1):
        @pl.when(position(way) < nz - 1)
        def _():
            for k in range(UNITS):
                z_copy((pr, plft)[way], unit(k), k, way, pz_send, pz_recv).wait_send()
            for k in range(nr):
                z_copy((wr, wl)[way], k, k, way, wz_send, wz_recv).wait_send()
    store.wait()


def on_device(n, nr, panel, centres_cols, centres_rows, diag_inverse, trailing):
    blk, width = centres_cols.shape
    quarter = blk // nr
    per = centres_rows.shape[0]
    group = per * n
    dma = pltpu.SemaphoreType.DMA
    vmem = pl.BlockSpec(memory_space=pltpu.VMEM)
    hbm = pl.BlockSpec(memory_space=pltpu.HBM)
    return pl.pallas_call(
        functools.partial(kernel, n, nr),
        out_shape=jax.ShapeDtypeStruct(trailing.shape, F32),
        in_specs=[hbm, hbm, vmem, hbm, hbm],
        out_specs=hbm,
        scratch_shapes=[
            pltpu.SMEM(panel.shape, jnp.int32),
            pltpu.VMEM(centres_cols.shape, BF16),
            pltpu.VMEM(diag_inverse.shape, F32),
            pltpu.VMEM(trailing.shape, F32),
            pltpu.VMEM((n, per, width), F32),
            pltpu.VMEM((group, width), F32),
            pltpu.VMEM((3, blk, blk), BF16),
            pltpu.VMEM((quarter // 2, width), BF16),
            pltpu.VMEM((quarter // 2, width), BF16),
            pltpu.VMEM((quarter // 2, width), BF16),
            pltpu.VMEM((quarter // 2, width), BF16),
            pltpu.VMEM((quarter // 2, width), BF16),
            pltpu.VMEM((nr, group, quarter), F32),
            pltpu.VMEM((nr, group, quarter), F32),
            pltpu.VMEM((nr, group, quarter), F32),
            pltpu.VMEM((nr, group, quarter), F32),
            pltpu.VMEM((nr, group, quarter), F32),
            pltpu.VMEM((quarter, blk), F32),
            pltpu.VMEM((nr, group, blk), F32),
            pltpu.VMEM((nr, group, blk), F32),
            dma((4,)),
            dma((n,)), dma((n,)),
            dma((UNITS,)), dma((UNITS,)),
            dma((2, UNITS)), dma((2, UNITS)),
            dma((UNITS,)), dma((UNITS,)),
            dma((nr,)), dma((nr,)),
            dma((nr,)), dma((nr,)),
            dma((2, nr)), dma((2, nr)),
            dma((nr,)), dma((nr,)),
        ],
        compiler_params=pltpu.CompilerParams(
            collective_id=0, has_side_effects=True, vmem_limit_bytes=VMEM_BYTES
        ),
    )(panel, centres_cols, centres_rows, diag_inverse, trailing)


def solution(mesh):
    return jax.shard_map(
        functools.partial(on_device, mesh.shape["col"], mesh.shape["row"]),
        mesh=mesh,
        in_specs=(P(), P("col", None), P(("row", "col"), None), P("col", None), P("row", "col")),
        out_specs=P("row", "col"),
        check_vma=False,
    )
```

```python
import functools
import math

import jax
import jax.numpy as jnp
from jax import lax
from jax.experimental import pallas as pl
from jax.experimental.pallas import tpu as pltpu
from jax.sharding import PartitionSpec as P

LAYERS = 3
EPS = 1e-06
UNITS = 4
HOP = UNITS
VMEM_BYTES = 63 * 2**20
MESH = pl.DeviceIdType.MESH
F32 = jnp.float32
BF16 = jnp.bfloat16
ACOS = tuple(
    v / math.pi
    for v in (
        1.5707963050, -0.2145988016, 0.0889789874, -0.0501743046,
        0.0308918810, -0.0170881256, 0.0066700901, -0.0012624911,
    )
)


def root(y):
    y = jnp.maximum(y, 1e-30)
    return y * lax.rsqrt(y)


def theta_of(u):
    rho = jnp.clip(u, -1.0, 1.0)
    theta = rho
    for layer in range(LAYERS):
        size = jnp.abs(rho) if layer == 0 else rho
        poly = jnp.full_like(size, ACOS[-1])
        for coef in ACOS[-2::-1]:
            poly = poly * size + coef
        low = root(1.0 - size)
        angle = low * poly
        sine = low * root(1.0 + size)
        if layer == 0:
            zero_order = jnp.where(rho < 0.0, angle, 1.0 - angle)
        else:
            zero_order = 1.0 - angle
        rho_next = sine * (1.0 / math.pi) + zero_order * rho
        theta = theta * zero_order + rho_next
        rho = rho_next
    return theta


def dot_t(a, b, precision=None):
    return lax.dot_general(
        a, b, (((1,), (1,)), ((), ())), precision=precision, preferred_element_type=F32
    )


def split3(a):
    hi = a.astype(BF16)
    rest = a - hi.astype(F32)
    mid = rest.astype(BF16)
    return hi, mid, (rest - mid.astype(F32)).astype(BF16)


def product3(a, weights, transposed):
    m = a.shape[0]
    terms = jnp.concatenate(split3(a), axis=0)
    dims = (((1,), (1 if transposed else 0,)), ((), ()))

    def mul(count, w):
        return lax.dot_general(terms[:count * m], w, dims, preferred_element_type=F32)

    p, q, t = mul(3, weights[0]), mul(2, weights[1]), mul(1, weights[2])
    small = t + q[m:] + p[2 * m:]
    return (small + (q[:m] + p[m:2 * m])) + p[:m]


def kernel(
    n, nr, panel_hbm, x_hbm, rows_ref, inv_hbm, trail_hbm, out_ref,
    panel, x_ref, inv_ref, trail_ref,
    rows_buf, rows_all, inv3, py, pr, plft, done, across, w_out, wo, wm, wr, wl, kt, part, part_in,
    in_sem, rows_send, rows_recv, py_send, py_recv, pz_send, pz_recv, cx_send, cx_recv,
    wo_send, wo_recv, wm_send, wm_recv, wz_send, wz_recv, pt_send, pt_recv,
):
    col = lax.axis_index("col")
    row = lax.axis_index("row")
    nz = n // 2
    z, y = col // 2, col % 2
    y_mate = z * 2 + 1 - y
    right, left = lax.rem(col + 2, n), lax.rem(col + n - 2, n)
    blk, width = x_ref.shape
    half = blk // 2
    quarter = blk // nr
    share = quarter // 2
    size = share // UNITS
    per = rows_ref.shape[0]

    barrier = pltpu.get_barrier_semaphore()

    def greet(**where):
        pl.semaphore_signal(barrier, inc=1, device_id=where, device_id_type=MESH)

    for d in range(1, n):
        greet(col=lax.rem(col + d, n))
    for d in range(1, nr):
        greet(row=lax.rem(row + d, nr))
        greet(row=lax.rem(row + d, nr), col=y_mate)
    loads = [
        pltpu.make_async_copy(src, dst, in_sem.at[i])
        for i, (src, dst) in enumerate(
            ((panel_hbm, panel), (x_hbm, x_ref), (inv_hbm, inv_ref), (trail_hbm, trail_ref))
        )
    ]
    for load in loads:
        load.start()
    rows_buf[col] = rows_ref[...].astype(F32)
    pl.semaphore_wait(barrier, n - 1 + 2 * (nr - 1))

    def remote(src, dst, send, recv, **where):
        return pltpu.make_async_remote_copy(
            src_ref=src, dst_ref=dst, send_sem=send, recv_sem=recv,
            device_id=where, device_id_type=MESH,
        )

    def rows_copy(d, slot):
        return remote(
            rows_buf.at[slot], rows_buf.at[slot], rows_send.at[d], rows_recv.at[slot],
            col=lax.rem(col + d, n),
        )

    for d in range(1, n):
        rows_copy(d, col).start()

    def unit(k):
        return pl.ds(pl.multiple_of(k * size, size), size)

    def own_unit(side, k):
        return pl.ds(pl.multiple_of(row * quarter + side * share + k * size, size), size)

    def py_copy(k):
        return remote(
            x_hbm.at[own_unit(1 - y, k)], py.at[unit(k)], py_send.at[k], py_recv.at[k], col=y_mate
        )

    def cx_copy(k):
        return remote(
            done.at[unit(k)], across.at[unit(k)], cx_send.at[k], cx_recv.at[k], col=y_mate
        )

    for k in range(UNITS):
        py_copy(k).start()
    for load in loads:
        load.wait()

    target = n // 4
    at = jnp.int32(0)
    for i in range(n):
        at = at + jnp.where(panel[i] == target, i, 0)
    root_here = at == col
    root_layer = at // 2 == z
    from_left = at // 2 <= z

    def block_kernel(a, a_f, x_norm):
        a_norm = jnp.sqrt(jnp.sum(a_f * a_f, axis=1, keepdims=True) + EPS)
        u = dot_t(a, x_ref[...]) * (1.0 / a_norm) * (1.0 / x_norm)
        return theta_of(u) * (a_norm * x_norm)

    def z_copy(buf, index, k, way, send, recv):
        return remote(
            buf.at[index], buf.at[index], send.at[way, k], recv.at[way, k],
            col=right if way == 0 else left,
        )

    def position(way):
        return z if way == 0 else nz - 1 - z

    def pass_on(buf, index, k, way, cand, send, recv):
        pos = position(way)

        @pl.when(pos == 0)
        def _():
            buf[index] = cand()

        @pl.when(pos > 0)
        def _():
            z_copy(buf, index, k, way, send, recv).wait_recv()
            buf[index] = lax.select(root_layer, cand(), buf[index])

        @pl.when(pos < nz - 1)
        def _():
            z_copy(buf, index, k, way, send, recv).start()

    def panel_slot(step):
        @pl.when(step < UNITS)
        def _():
            py_copy(step).wait_recv()
            own = x_ref[own_unit(y, step), :]
            py[unit(step), :] = lax.select(root_here, own, py[unit(step), :])

        for way, buf in enumerate((pr, plft)):
            k = step - HOP * position(way)

            @pl.when(jnp.logical_and(k >= 0, k < UNITS))
            def _():
                pass_on(buf, unit(k), k, way, lambda: py[unit(k), :], pz_send, pz_recv)

        k_done = step - HOP * (nz - 1)

        @pl.when(k_done >= 0)
        def _():
            sel = unit(k_done)
            done[sel, :] = lax.select(from_left, pr[sel, :], plft[sel, :])
            cx_copy(k_done).start()

    def slots(first, last):
        @pl.loop(first, last)
        def _(step):
            panel_slot(step)

    def panel_half(side, a):
        kt[pl.ds(pl.multiple_of(side * share, share), share), :] = block_kernel(a, a.astype(F32), x_norm)

    def work_rows():
        for d in range(1, n):
            slot = lax.rem(col + n - d, n)
            rows_copy(d, slot).wait_recv()
        for c in range(n):
            rows_all[c * per:(c + 1) * per, :] = rows_buf[c]
        a_f = rows_all[...]
        return block_kernel(a_f.astype(BF16), a_f, x_norm)

    def wo_copy(d, slot):
        peer = lax.rem(row + d, nr)
        return remote(w_out.at[peer], wo.at[slot], wo_send.at[d], wo_recv.at[slot], row=peer)

    def wm_copy(d, slot):
        peer = lax.rem(row + d, nr)
        return remote(
            w_out.at[peer], wm.at[slot], wm_send.at[d], wm_recv.at[slot], row=peer, col=y_mate
        )

    def work_mid(a):
        low = product3(a[:, :half], [inv3[i, :half, :half] for i in range(3)], True)
        high = product3(a, [inv3[i, half:, :] for i in range(3)], True)
        return jnp.concatenate([low, high], axis=1)

    def work_w(mid):
        low = product3(mid, [inv3[i, :, :half] for i in range(3)], False)
        high = product3(mid[:, half:], [inv3[i, half:, half:] for i in range(3)], False)
        w = jnp.concatenate([low, high], axis=1)
        for j in range(nr):
            w_out[j] = w[:, j * quarter:(j + 1) * quarter]
        for d in range(nr):
            wm_copy(d, row).start()
        for d in range(1, nr):
            wo_copy(d, row).start()
        wo[row] = w_out[row]

    def work_exchange():
        for d in range(nr):
            slot = lax.rem(row + nr - d, nr)
            wm_copy(d, slot).wait_recv()
        for d in range(1, nr):
            slot = lax.rem(row + nr - d, nr)
            wo_copy(d, slot).wait_recv()
        for k in range(nr):
            wm[k] = lax.select(root_here, wo[k], wm[k])

    def w_hop(step):
        for way, buf in enumerate((wr, wl)):
            @pl.when(position(way) == step)
            def _():
                for k in range(nr):
                    pass_on(buf, k, k, way, lambda: wm[k], wz_send, wz_recv)

    slots(0, HOP)

    sums = jnp.zeros((blk, 128), F32)
    for j in range(0, width, 128):
        piece = x_ref[:, j:j + 128].astype(F32)
        sums = sums + piece * piece
    x_norm = jnp.sqrt(jnp.sum(sums.T, axis=0, keepdims=True) + EPS)
    for i, term in enumerate(split3(inv_ref[...])):
        inv3[i] = term

    k_rows = work_rows()
    slots(HOP, 2 * HOP)
    work_w(work_mid(k_rows))
    slots(2 * HOP, 3 * HOP)
    work_exchange()
    w_hop(0)
    slots(3 * HOP, nz * HOP)
    w_hop(1)
    panel_half(y, done[...])
    w_hop(2)
    for k in range(UNITS):
        cx_copy(k).wait_recv()
    panel_half(1 - y, across[...])

    @pl.loop(3, nz)
    def _(step):
        w_hop(step)

    def part_copy(d, slot):
        peer = lax.rem(row + d, nr)
        return remote(part.at[peer], part_in.at[slot], pt_send.at[d], pt_recv.at[slot], row=peer)

    w = jnp.concatenate([lax.select(from_left, wr[j], wl[j]) for j in range(nr)], axis=0)
    update = jnp.dot(w, kt[...], precision=lax.Precision.HIGHEST, preferred_element_type=F32)
    group = update.shape[0] // nr
    for j in range(nr):
        part[j] = update[j * group:(j + 1) * group]
    for d in range(1, nr):
        part_copy(d, row).start()
    total = part[row]
    for d in range(1, nr):
        slot = lax.rem(row + nr - d, nr)
        part_copy(d, slot).wait_recv()
        total = total + part_in[slot]
    trail = trail_ref[...]
    trail_ref[...] = lax.select(panel[col] > target, trail - total, trail)
    store = pltpu.make_async_copy(trail_ref, out_ref, in_sem.at[0])
    store.start()

    for d in range(1, n):
        rows_copy(d, col).wait_send()
    for k in range(UNITS):
        py_copy(k).wait_send()
        cx_copy(k).wait_send()
    for d in range(nr):
        wm_copy(d, row).wait_send()
    for d in range(1, nr):
        wo_copy(d, row).wait_send()
        part_copy(d, row).wait_send()
    for way in (0, 1):
        @pl.when(position(way) < nz - 1)
        def _():
            for k in range(UNITS):
                z_copy((pr, plft)[way], unit(k), k, way, pz_send, pz_recv).wait_send()
            for k in range(nr):
                z_copy((wr, wl)[way], k, k, way, wz_send, wz_recv).wait_send()
    store.wait()


def on_device(n, nr, panel, centres_cols, centres_rows, diag_inverse, trailing):
    blk, width = centres_cols.shape
    quarter = blk // nr
    per = centres_rows.shape[0]
    group = per * n
    dma = pltpu.SemaphoreType.DMA
    vmem = pl.BlockSpec(memory_space=pltpu.VMEM)
    hbm = pl.BlockSpec(memory_space=pltpu.HBM)
    return pl.pallas_call(
        functools.partial(kernel, n, nr),
        out_shape=jax.ShapeDtypeStruct(trailing.shape, F32),
        in_specs=[hbm, hbm, vmem, hbm, hbm],
        out_specs=hbm,
        scratch_shapes=[
            pltpu.SMEM(panel.shape, jnp.int32),
            pltpu.VMEM(centres_cols.shape, BF16),
            pltpu.VMEM(diag_inverse.shape, F32),
            pltpu.VMEM(trailing.shape, F32),
            pltpu.VMEM((n, per, width), F32),
            pltpu.VMEM((group, width), F32),
            pltpu.VMEM((3, blk, blk), BF16),
            pltpu.VMEM((quarter // 2, width), BF16),
            pltpu.VMEM((quarter // 2, width), BF16),
            pltpu.VMEM((quarter // 2, width), BF16),
            pltpu.VMEM((quarter // 2, width), BF16),
            pltpu.VMEM((quarter // 2, width), BF16),
            pltpu.VMEM((nr, group, quarter), F32),
            pltpu.VMEM((nr, group, quarter), F32),
            pltpu.VMEM((nr, group, quarter), F32),
            pltpu.VMEM((nr, group, quarter), F32),
            pltpu.VMEM((nr, group, quarter), F32),
            pltpu.VMEM((quarter, blk), F32),
            pltpu.VMEM((nr, group, blk), F32),
            pltpu.VMEM((nr, group, blk), F32),
            dma((4,)),
            dma((n,)), dma((n,)),
            dma((UNITS,)), dma((UNITS,)),
            dma((2, UNITS)), dma((2, UNITS)),
            dma((UNITS,)), dma((UNITS,)),
            dma((nr,)), dma((nr,)),
            dma((nr,)), dma((nr,)),
            dma((2, nr)), dma((2, nr)),
            dma((nr,)), dma((nr,)),
        ],
        compiler_params=pltpu.CompilerParams(
            collective_id=0, has_side_effects=True, vmem_limit_bytes=VMEM_BYTES
        ),
    )(panel, centres_cols, centres_rows, diag_inverse, trailing)


def solution(mesh):
    return jax.shard_map(
        functools.partial(on_device, mesh.shape["col"], mesh.shape["row"]),
        mesh=mesh,
        in_specs=(P(), P("col", None), P(("row", "col"), None), P("col", None), P("row", "col")),
        out_specs=P("row", "col"),
        check_vma=False,
    )
```
